32 devices in a mesh: seq: 8 (over z, y), head: 4 (over x, core).
Axes of the slice: x: 2, y: 2, z: 4, core: 2. Of those that a mesh axis runs over, the one named last changes fastest.
Arguments:
- queries: bfloat16 [8192, 32, 128], P('seq', 'head'), may hold values from -0.59765625 to 0.59765625
- keys: bfloat16 [8192, 32, 128], P('seq', 'head'), may hold values from -6 to 6
- values: bfloat16 [8192, 32, 128], P('seq', 'head'), may hold values from -6 to 6
- log_decay: float32 [8192, 32], P('seq', 'head'), may hold values from -0.8 to 0, as said below
- level_weight: float32 [8192, 32, 8], P('seq', 'head'), may hold values from 0.1 to 2
- norm_gain: float32 [32, 128], P('head'), may hold values from 0.25 to 1.75
- out_weight: bfloat16 [4096, 4096], P('head'), may hold values from -0.09375 to 0.09375
Outputs:
- mixed: bfloat16 [8192, 4096], P(('seq', 'head'))
The draws below stay inside these ranges and needn't reach their ends.
Inputs may be any that keep to these rules, and one draw needn't show every extreme that they name: `log_decay`: negative logarithms of decay factors.
All inputs are finite; a program needn't handle non-finite values.
Results may differ from the reference program's by a relative error of at most 0.023.
Values may be sent and summed in bfloat16 or wider, within the bound.
A program may use at most 128 MiB of HBM per device.

```python
import math
import jax
import jax.numpy as jnp
import numpy as np
from jax import lax

D = 4096
HEAD_TOTAL = 32
HD = 128
SPAN = 64
TOK_DEV = 1024
LEVELS = 8
TOKEN_TOTAL = 8192
N_HEAD = 4


def decay_law(key, fast_share):
    variety_random_key, quick_random_key, gradual_random_key, block_random_key, token_random_key, spike_random_key, forget_random_key = jax.random.split(key, 7)
    fast_heads = jax.random.uniform(variety_random_key, (HEAD_TOTAL,)) < fast_share
    fast_rate = jnp.exp(jax.random.uniform(quick_random_key, (HEAD_TOTAL,), minval=math.log(1.0 / 50.0), maxval=math.log(1.0 / 30.0)))
    slow_rate = math.log(10.0) / TOKEN_TOTAL * jax.random.uniform(gradual_random_key, (HEAD_TOTAL,), minval=0.1, maxval=0.5)
    decay_speed = jnp.where(fast_heads, fast_rate, slow_rate)
    block_multiplier = jnp.exp(jax.random.uniform(block_random_key, (TOKEN_TOTAL // TOK_DEV, HEAD_TOTAL), minval=math.log(0.5), maxval=math.log(2.0)))
    block_multiplier = jnp.repeat(block_multiplier, TOK_DEV, axis=0)
    token_multiplier = jax.random.uniform(token_random_key, (TOKEN_TOTAL, HEAD_TOTAL), minval=0.5, maxval=1.5)
    decay_spikes = jax.random.uniform(spike_random_key, (TOKEN_TOTAL, HEAD_TOTAL)) < 2.0 / TOKEN_TOTAL
    forget_amount = jnp.log(jax.random.uniform(forget_random_key, (TOKEN_TOTAL, HEAD_TOTAL), minval=0.5, maxval=0.8))
    return -(decay_speed[None, :] * block_multiplier * token_multiplier) + jnp.where(decay_spikes, forget_amount, 0.0)


def draw_log_decay(key, part):
    key = jax.random.fold_in(key, 11)
    return decay_law(key, 0.5).astype(jnp.float32)


def steps_of(own_key, extent, shards, smallest, high):
    loudness, own = 1.0, jax.random.fold_in(own_key, 6)
    for dim, parts in shards:
        draws = jnp.exp(jax.random.uniform(jax.random.fold_in(own, dim), (parts,), jnp.float32, smallest / len(shards), high / len(shards)))
        loudness = loudness * jnp.repeat(draws, extent[dim] // parts).reshape([-1 if axis == dim else 1 for axis in range(len(extent))])
    return loudness


def noise(key, extent, deviation, bound, cuts=(), kind=jnp.bfloat16):
    entries = jax.random.normal(key, extent, jnp.float32) * deviation
    if len(cuts) > 0:
        entries = steps_of(key, extent, cuts, -0.22, 0.18) * entries
    return jnp.clip(entries, min=-bound, max=bound).astype(kind)


def setup_inputs(seed: int = 0) -> dict:
    key_of = jax.random.split(jax.random.key(seed), 8)
    return {
        "queries": noise(key_of[0], (TOKEN_TOTAL, HEAD_TOTAL, HD), 0.0884, 0.59765625, ((0, 8), (1, 4))),
        "keys": noise(key_of[1], (TOKEN_TOTAL, HEAD_TOTAL, HD), 1.0, 6.0, ((0, 8), (1, 4))),
        "values": noise(key_of[2], (TOKEN_TOTAL, HEAD_TOTAL, HD), 1.0, 6.0, ((0, 8), (1, 4))),
        "log_decay": draw_log_decay(jax.random.fold_in(key_of[7], 71), 0),
        "level_weight": jnp.clip(jnp.exp(math.log(2.0) - 2.9957323 * jax.random.uniform(key_of[4], (TOKEN_TOTAL, HEAD_TOTAL, LEVELS), jnp.float32) ** steps_of(key_of[4], (TOKEN_TOTAL, HEAD_TOTAL, LEVELS), ((0, 8), (1, 4)), -0.2, 0.2)), 0.1, 2.0),
        "norm_gain": jnp.clip(1.0 + 0.15 * jax.random.normal(key_of[5], (HEAD_TOTAL, HD), jnp.float32), 0.25, 1.75),
        "out_weight": noise(key_of[6], (HEAD_TOTAL * HD, D), (HEAD_TOTAL * HD) ** -0.5, 0.09375, ((0, 4),)),
    }


def span_terms(query_blocks, key_blocks, value_blocks, inner):
    size = inner.shape[1]
    scores = jnp.einsum('cthd,cshd->chts', query_blocks.astype(jnp.float32), key_blocks.astype(jnp.float32))
    leading = jnp.transpose(inner, (0, 2, 1))
    causal = np.tril(np.ones((size, size), dtype=bool))
    spread = jnp.where(causal, leading[:, :, :, None] - leading[:, :, None, :], 0.0)
    weight = jnp.where(causal, jnp.exp(spread), 0.0)
    probs = lax.optimization_barrier((scores * weight).astype(jnp.bfloat16))
    within = jnp.einsum('chts,cshe->cthe', probs.astype(jnp.float32), value_blocks.astype(jnp.float32))
    scaled = jnp.exp(inner[:, -1:, :] - inner)[:, :, :, None] * key_blocks.astype(jnp.float32)
    scaled = lax.optimization_barrier(scaled.astype(jnp.bfloat16))
    states = jnp.einsum('cshd,cshe->chde', scaled.astype(jnp.float32), value_blocks.astype(jnp.float32))
    return (within, states)

def level_terms(query_blocks, inner, states, totals, before, weights):
    count = states.shape[0]
    depth = count.bit_length() - 1
    output = jnp.zeros(query_blocks.shape, jnp.float32)
    blocks = states
    block_total = totals
    span_ids = np.arange(count)
    for level_now in range(1, depth + 1):
        shift_by = level_now - 1
        present = (span_ids >> shift_by & 1).astype(np.float32)
        source = np.maximum((span_ids >> shift_by) - 1, 0)
        middle = span_ids >> shift_by << shift_by
        picked = lax.optimization_barrier(blocks[source].astype(jnp.bfloat16))
        readout = jnp.einsum('cthd,chde->cthe', query_blocks.astype(jnp.float32), picked.astype(jnp.float32))
        factor = jnp.exp((before - before[middle])[:, None, :] + inner) * weights[:, :, :, level_now] * present[:, None, None]
        output = output + factor[:, :, :, None] * readout
        blocks = jnp.exp(block_total[1::2])[:, :, None, None] * blocks[0::2] + blocks[1::2]
        block_total = block_total[0::2] + block_total[1::2]
    return output

def reference(queries, keys, values, log_decay, level_weight, norm_gain, out_weight):
    count = TOKEN_TOTAL // SPAN

    def per_head(items):
        query_one, key_one, value_one, decay_one, weight_one = items
        shaped = (count, SPAN, 1, HD)
        query_blocks = query_one.reshape(shaped)
        key_blocks = key_one.reshape(shaped)
        value_blocks = value_one.reshape(shaped)
        weights = weight_one.reshape(count, SPAN, 1, LEVELS)
        inner = jnp.cumsum(decay_one.reshape(count, SPAN, 1), axis=1)
        totals = inner[:, -1, :]
        before = jnp.cumsum(totals, axis=0) - totals
        within, states = span_terms(query_blocks, key_blocks, value_blocks, inner)
        output = within * weights[:, :, :, 0:1]
        output = output + level_terms(query_blocks, inner, states, totals, before, weights)
        return output.reshape(TOKEN_TOTAL, HD)
    attention = lax.map(per_head, (jnp.transpose(queries, (1, 0, 2)), jnp.transpose(keys, (1, 0, 2)), jnp.transpose(values, (1, 0, 2)), jnp.transpose(log_decay, (1, 0)), jnp.transpose(level_weight, (1, 0, 2))))
    attention = jnp.transpose(attention, (1, 0, 2))
    mean_square = lax.optimization_barrier(jnp.mean(attention * attention, axis=-1, keepdims=True))
    normed = (attention * lax.rsqrt(mean_square + 1e-06) * norm_gain[None]).astype(jnp.bfloat16)
    normed = normed.reshape(TOKEN_TOTAL, HEAD_TOTAL * HD)
    group_width = HEAD_TOTAL // N_HEAD * HD
    summed = jnp.zeros((TOKEN_TOTAL, D), jnp.float32)
    for group_index in range(N_HEAD):
        lower_col = group_index * group_width
        partial_sum = jnp.dot(normed[:, lower_col:lower_col + group_width], out_weight[lower_col:lower_col + group_width], preferred_element_type=jnp.float32)
        partial_sum = lax.optimization_barrier(partial_sum.astype(jnp.bfloat16))
        summed = summed + partial_sum.astype(jnp.float32)
    return summed.astype(jnp.bfloat16)
```

```python
import functools

import jax
import jax.numpy as jnp
from jax import lax
from jax.experimental import pallas as pl
from jax.experimental.pallas import tpu as pltpu
from jax.sharding import PartitionSpec as P

SPAN = 64
QUAD = 4 * SPAN
PIECES = 4
F32 = jnp.float32
BF16 = jnp.bfloat16
HIGH = lax.Precision.HIGHEST
MESH = pl.DeviceIdType.MESH


def kernel(
    chips, bits, heads, levels, width,
    q_hbm, k_hbm, v_hbm, w_hbm, ld_ref, ldt_ref, lw_ref, gain_ref, out_ref,
    q, k, v, w, cum, cumt, tots, state, lev, attn, normed,
    summary, sum_send, sum_recv, tot_send, tot_recv, far,
    core_send, core_recv, x_send, x_recv, acc,
    in_sem, ss_sem, sr_sem, ts_sem, tr_sem, cs_sem, cr_sem, xs_sem, xr_sem,
):
    rows_all = q.shape[0]
    quads = rows_all // QUAD
    block = out_ref.shape[0]
    group = 2 * block
    piece_cols = out_ref.shape[1] // PIECES
    position = lax.axis_index("seq")
    head_id = lax.axis_index("head")
    chip = head_id // 2
    core = head_id % 2
    other_core = chip * 2 + (1 - core)

    loads = [
        pltpu.make_async_copy(src, dst, in_sem.at[n])
        for n, (src, dst) in enumerate(((k_hbm, k), (v_hbm, v), (q_hbm, q), (w_hbm, w)))
    ]
    for load in loads:
        load.start()

    bit_of = [(position // (1 << b)) % 2 for b in range(bits)]
    partner_of = [position + (1 - 2 * bit_of[b]) * (1 << b) for b in range(bits)]
    chip_of = [(chip + 1 + i) % chips for i in range(chips)]

    barrier = pltpu.get_barrier_semaphore()
    for b in range(bits):
        pl.semaphore_signal(barrier, inc=1, device_id={"seq": partner_of[b]}, device_id_type=MESH)
    pl.semaphore_signal(barrier, inc=1, device_id={"head": other_core}, device_id_type=MESH)
    for i in range(chips - 1):
        pl.semaphore_signal(
            barrier, inc=1, device_id={"head": chip_of[i] * 2 + core}, device_id_type=MESH
        )
    pl.semaphore_wait(barrier, bits + chips)

    row_id = lax.broadcasted_iota(jnp.int32, (QUAD, QUAD), 0)
    col_id = lax.broadcasted_iota(jnp.int32, (QUAD, QUAD), 1)

    def head_cols(h):
        return slice(h * width, (h + 1) * width)

    def quad_rows(c):
        return pl.ds(pl.multiple_of(c * QUAD, QUAD), QUAD)

    loads[0].wait()
    loads[1].wait()

    @pl.loop(0, quads)
    def _(c):
        rows = quad_rows(c)
        lower = (row_id >= col_id).astype(F32)
        upper = (row_id <= col_id).astype(F32)
        cq = jnp.dot(lower, ld_ref[rows, :], precision=HIGH, preferred_element_type=F32)
        cum[rows, :] = cq
        cumt[c] = jnp.dot(ldt_ref[c], upper, precision=HIGH, preferred_element_type=F32)
        last = cq[QUAD - 1 : QUAD, :]
        tots[c] = jnp.broadcast_to(last, (8, 128))
        decay = jnp.exp(last - cq)
        for h in range(heads):
            hs = head_cols(h)
            scaled = (k[rows, hs].astype(F32) * decay[:, h : h + 1]).astype(BF16)
            state[c, h] = lax.dot_general(
                scaled, v[rows, hs], (((0,), (0,)), ((), ())), preferred_element_type=F32
            )

    t = [tots[c][0:1, :] for c in range(quads)]
    e1, e3, e23 = jnp.exp(t[1]), jnp.exp(t[3]), jnp.exp(t[2] + t[3])
    total = t[0] + t[1] + t[2] + t[3]
    offset = jnp.zeros_like(total)
    before = [jnp.zeros_like(total), t[0], t[0] + t[1], t[0] + t[1] + t[2]]
    nothing = jnp.zeros((width, width), BF16)
    for h in range(heads):
        s0, s2 = state[0, h], state[2, h]
        low = e1[:, h : h + 1] * s0 + state[1, h]
        whole = e23[:, h : h + 1] * low + e3[:, h : h + 1] * s2 + state[3, h]
        summary[h] = whole
        sum_send[0, h] = whole.astype(BF16)
        low_b = low.astype(BF16)
        lev[0, h, :, :width] = nothing
        lev[0, h, :, width:] = nothing
        lev[1, h, :, :width] = s0.astype(BF16)
        lev[1, h, :, width:] = nothing
        lev[2, h, :, :width] = nothing
        lev[2, h, :, width:] = low_b
        lev[3, h, :, :width] = s2.astype(BF16)
        lev[3, h, :, width:] = low_b
    tot_send[0] = jnp.broadcast_to(total, (8, 128))

    def exchange(b):
        return (
            pltpu.make_async_remote_copy(
                sum_send.at[b], sum_recv.at[b], ss_sem.at[b], sr_sem.at[b],
                device_id={"seq": partner_of[b]}, device_id_type=MESH,
            ),
            pltpu.make_async_remote_copy(
                tot_send.at[b], tot_recv.at[b], ts_sem.at[b], tr_sem.at[b],
                device_id={"seq": partner_of[b]}, device_id_type=MESH,
            ),
        )

    for copy in exchange(0):
        copy.start()

    loads[2].wait()

    def local_quad(c):
        rows = quad_rows(c)
        cq = cum[rows, :]
        ecq = jnp.exp(cq)
        ct = cumt[c]
        lwq = lw_ref[rows, :]
        is_last = (c == quads - 1).astype(F32)
        g4 = is_last * jnp.exp(t[2]) + (1.0 - is_last)
        causal = row_id >= col_id
        same = (row_id // SPAN) == (col_id // SPAN)
        near = (row_id // (2 * SPAN)) == (col_id // (2 * SPAN))
        for h in range(heads):
            hs = head_cols(h)
            at = h * levels
            qh = q[rows, hs]
            s = lax.dot_general(
                qh, k[rows, hs], (((1,), (1,)), ((), ())), preferred_element_type=F32
            )
            spread = jnp.where(causal, cq[:, h : h + 1] - ct[h : h + 1, :], -1e30)
            weight = jnp.where(
                same,
                lwq[:, at : at + 1],
                jnp.where(near, lwq[:, at + 1 : at + 2], lwq[:, at + 2 : at + 3]),
            )
            probs = (s * jnp.exp(spread) * weight).astype(BF16)
            o = jnp.dot(probs, v[rows, hs], preferred_element_type=F32)
            read = jnp.dot(qh, lev[c, h], preferred_element_type=F32)
            col = ecq[:, h : h + 1]
            o = o + (col * lwq[:, at + 3 : at + 4]) * read[:, :width]
            o = o + (col * lwq[:, at + 4 : at + 5] * g4[:, h : h + 1]) * read[:, width:]
            attn[rows, hs] = o

    far_gain = []
    for b in range(bits):
        first, last = b * quads // bits, (b + 1) * quads // bits

        @pl.loop(first, last)
        def _(c):
            local_quad(c)

        for copy in exchange(b):
            copy.wait()
        flag = bit_of[b].astype(F32)
        other = tot_recv[b][0:1, :]
        far_gain.append(flag * jnp.exp(offset))
        mine_by = flag + (1.0 - flag) * jnp.exp(other)
        other_by = flag * jnp.exp(total) + (1.0 - flag)
        for h in range(heads):
            got = sum_recv[b, h]
            far[h, :, b * width : (b + 1) * width] = got
            if b < bits - 1:
                joint = (
                    mine_by[:, h : h + 1] * summary[h]
                    + other_by[:, h : h + 1] * got.astype(F32)
                )
                summary[h] = joint
                sum_send[b + 1, h] = joint.astype(BF16)
        offset = offset + flag * other
        total = total + other
        if b < bits - 1:
            tot_send[b + 1] = jnp.broadcast_to(total, (8, 128))
            for copy in exchange(b + 1):
                copy.start()

    loads[3].wait()

    def finish_quad(c, at_row):
        rows = quad_rows(c)
        ecq = jnp.exp(cum[rows, :])
        lwq = lw_ref[rows, :]
        lead = jnp.zeros_like(before[0])
        for n in range(1, quads):
            lead = lead + (c == n).astype(F32) * before[n]
        lead = jnp.exp(lead)
        for h in range(heads):
            hs = head_cols(h)
            read = jnp.dot(q[rows, hs], far[h], preferred_element_type=F32)
            o = attn[rows, hs]
            col = ecq[:, h : h + 1]
            for b in range(bits):
                at = h * levels + 5 + b
                gain = (lead * far_gain[b])[:, h : h + 1]
                o = o + (col * lwq[:, at : at + 1] * gain) * read[:, b * width : (b + 1) * width]
            mean_square = jnp.mean(o * o, axis=-1, keepdims=True)
            o = o * lax.rsqrt(mean_square + 1e-6) * gain_ref[h : h + 1, :]
            normed[pl.ds(pl.multiple_of(at_row, QUAD), QUAD), hs] = o.astype(BF16)

    def to_core(i, j):
        return pltpu.make_async_remote_copy(
            core_send.at[i, j], core_recv.at[i, j], cs_sem.at[i, j], cr_sem.at[i, j],
            device_id={"head": other_core}, device_id_type=MESH,
        )

    def to_chip(i, j):
        return pltpu.make_async_remote_copy(
            x_send.at[i, j], x_recv.at[i, j], xs_sem.at[i, j], xr_sem.at[i, j],
            device_id={"head": chip_of[i] * 2 + core}, device_id_type=MESH,
        )

    def product(which, j):
        rows = pl.ds(pl.multiple_of(which * block, block), block)
        cols = pl.ds(pl.multiple_of(j * piece_cols, piece_cols), piece_cols)
        return jnp.dot(normed[rows, :], w[:, cols], preferred_element_type=F32)

    per_group = group // QUAD
    for i in range(chips):

        @pl.loop(0, per_group)
        def _(n):
            finish_quad(chip_of[i] * per_group + n, n * QUAD)

        @pl.loop(0, PIECES + 1)
        def _(j):
            @pl.when(j < PIECES)
            def _():
                core_send[i, j] = product(1 - core, j).astype(BF16)
                to_core(i, j).start()

            @pl.when(j > 0)
            def _():
                mine = product(core, j - 1)
                to_core(i, j - 1).wait()
                mine = mine + core_recv[i, j - 1].astype(F32)
                if i < chips - 1:
                    x_send[i, j - 1] = mine.astype(BF16)
                    to_chip(i, j - 1).start()
                else:
                    acc[j - 1] = mine

    @pl.loop(0, PIECES)
    def _(j):
        mine = acc[j]
        for i in range(chips - 1):
            to_chip(i, j).wait()
            mine = mine + x_recv[i, j].astype(F32)
        cols = pl.ds(pl.multiple_of(j * piece_cols, piece_cols), piece_cols)
        out_ref[:, cols] = mine.astype(BF16)


def body(chips, bits, queries, keys, values, log_decay, level_weight, norm_gain, out_weight):
    rows, heads, width = queries.shape
    levels = level_weight.shape[2]
    depth, columns = out_weight.shape
    block = rows // (2 * chips)
    quads = rows // QUAD
    flat = (rows, heads * width)
    piece = (PIECES, block, columns // PIECES)
    decay = jnp.pad(log_decay, ((0, 0), (0, 128 - heads)))
    decay_t = jnp.transpose(log_decay.reshape(quads, QUAD, heads), (0, 2, 1))
    vmem = pl.BlockSpec(memory_space=pltpu.VMEM)
    hbm = pl.BlockSpec(memory_space=pl.ANY)
    dma = pltpu.SemaphoreType.DMA
    return pl.pallas_call(
        functools.partial(kernel, chips, bits, heads, levels, width),
        out_shape=jax.ShapeDtypeStruct((block, columns), BF16),
        in_specs=[hbm] * 4 + [vmem] * 4,
        out_specs=vmem,
        scratch_shapes=[
            pltpu.VMEM(flat, BF16),
            pltpu.VMEM(flat, BF16),
            pltpu.VMEM(flat, BF16),
            pltpu.VMEM((depth, columns), BF16),
            pltpu.VMEM((rows, 128), F32),
            pltpu.VMEM((quads, heads, QUAD), F32),
            pltpu.VMEM((quads, 8, 128), F32),
            pltpu.VMEM((quads, heads, width, width), F32),
            pltpu.VMEM((quads, heads, width, 2 * width), BF16),
            pltpu.VMEM(flat, F32),
            pltpu.VMEM((2 * block, heads * width), BF16),
            pltpu.VMEM((heads, width, width), F32),
            pltpu.VMEM((bits, heads, width, width), BF16),
            pltpu.VMEM((bits, heads, width, width), BF16),
            pltpu.VMEM((bits, 8, 128), F32),
            pltpu.VMEM((bits, 8, 128), F32),
            pltpu.VMEM((heads, width, bits * width), BF16),
            pltpu.VMEM((chips,) + piece, BF16),
            pltpu.VMEM((chips,) + piece, BF16),
            pltpu.VMEM((chips - 1,) + piece, BF16),
            pltpu.VMEM((chips - 1,) + piece, BF16),
            pltpu.VMEM(piece, F32),
            dma((4,)),
            dma((bits,)),
            dma((bits,)),
            dma((bits,)),
            dma((bits,)),
            dma((chips, PIECES)),
            dma((chips, PIECES)),
            dma((chips - 1, PIECES)),
            dma((chips - 1, PIECES)),
        ],
        compiler_params=pltpu.CompilerParams(
            collective_id=0, has_side_effects=True, vmem_limit_bytes=58 * 1024 * 1024
        ),
    )(
        queries.reshape(flat),
        keys.reshape(flat),
        values.reshape(flat),
        out_weight,
        decay,
        decay_t,
        level_weight.reshape(rows, heads * levels),
        norm_gain,
    )


def solution(mesh):
    chips = mesh.shape["head"] // 2
    bits = mesh.shape["seq"].bit_length() - 1
    return jax.shard_map(
        functools.partial(body, chips, bits),
        mesh=mesh,
        in_specs=(
            P("seq", "head", None),
            P("seq", "head", None),
            P("seq", "head", None),
            P("seq", "head"),
            P("seq", "head", None),
            P("head", None),
            P("head", None),
        ),
        out_specs=P(("seq", "head"), None),
        check_vma=False,
    )
```

```python
import functools

import jax
import jax.numpy as jnp
from jax import lax
from jax.experimental import pallas as pl
from jax.experimental.pallas import tpu as pltpu
from jax.sharding import PartitionSpec as P

SPAN = 64
QUAD = 4 * SPAN
PIECES = 4
PARTS = 4
F32 = jnp.float32
BF16 = jnp.bfloat16
HIGH = lax.Precision.HIGHEST
MESH = pl.DeviceIdType.MESH


def kernel(
    chips, bits, heads, levels, width,
    q_hbm, k_hbm, v_hbm, w_hbm, ldt_ref, lwt_ref, gain_ref, out_ref, x_recv,
    q, k, v, w, cum, cumt, lw_ref, tots, state, lev, attn, normed,
    summary, sum_send, sum_recv, tot_send, tot_recv, far,
    core_send, core_recv, x_send, acc,
    in_sem, ss_sem, sr_sem, ts_sem, tr_sem, cs_sem, cr_sem, xs_sem, xr_sem, out_sem,
):
    rows_all = q.shape[0]
    quads = rows_all // QUAD
    block = out_ref.shape[0]
    group = 2 * block
    piece_cols = out_ref.shape[1] // PIECES
    per_part = heads // PARTS
    position = lax.axis_index("seq")
    head_id = lax.axis_index("head")
    chip = head_id // 2
    core = head_id % 2
    other_core = chip * 2 + (1 - core)

    loads = [
        pltpu.make_async_copy(src, dst, in_sem.at[n])
        for n, (src, dst) in enumerate(((k_hbm, k), (v_hbm, v), (q_hbm, q), (w_hbm, w)))
    ]
    loads[0].start()
    loads[1].start()

    bit_of = [(position // (1 << b)) % 2 for b in range(bits)]
    partner_of = [position + (1 - 2 * bit_of[b]) * (1 << b) for b in range(bits)]
    chip_of = [(chip + 1 + i) % chips for i in range(chips)]

    barrier = pltpu.get_barrier_semaphore()
    for b in range(bits):
        pl.semaphore_signal(barrier, inc=1, device_id={"seq": partner_of[b]}, device_id_type=MESH)
    pl.semaphore_signal(barrier, inc=1, device_id={"head": other_core}, device_id_type=MESH)
    for i in range(chips - 1):
        pl.semaphore_signal(
            barrier, inc=1, device_id={"head": chip_of[i] * 2 + core}, device_id_type=MESH
        )
    pl.semaphore_wait(barrier, bits + chips)

    row_id = lax.broadcasted_iota(jnp.int32, (QUAD, QUAD), 0)
    col_id = lax.broadcasted_iota(jnp.int32, (QUAD, QUAD), 1)

    def head_cols(h):
        return slice(h * width, (h + 1) * width)

    def quad_rows(c):
        return pl.ds(pl.multiple_of(c * QUAD, QUAD), QUAD)

    @pl.loop(0, quads)
    def _(c):
        rows = quad_rows(c)
        lower = (row_id >= col_id).astype(F32)
        upper = (row_id <= col_id).astype(F32)
        decay = ldt_ref[:, rows]
        cumt[c] = jnp.dot(decay, upper, precision=HIGH, preferred_element_type=F32)
        wide = jnp.concatenate([decay, jnp.zeros((128 - heads, QUAD), F32)], axis=0)
        cq = lax.dot_general(
            lower, wide, (((1,), (1,)), ((), ())), precision=HIGH, preferred_element_type=F32
        )
        cum[rows, :] = cq
        tots[c] = jnp.broadcast_to(cq[QUAD - 1 : QUAD, :], (8, 128))
        lw_ref[rows, :] = jnp.transpose(lwt_ref[:, rows])

    t = [tots[c][0:1, :] for c in range(quads)]
    e1, e3, e23 = jnp.exp(t[1]), jnp.exp(t[3]), jnp.exp(t[2] + t[3])
    total = t[0] + t[1] + t[2] + t[3]
    before = [jnp.zeros_like(total), t[0], t[0] + t[1], t[0] + t[1] + t[2]]
    tot_send[0] = jnp.broadcast_to(total, (8, 128))

    def exchange_total(b):
        return pltpu.make_async_remote_copy(
            tot_send.at[b], tot_recv.at[b], ts_sem.at[b], tr_sem.at[b],
            device_id={"seq": partner_of[b]}, device_id_type=MESH,
        )

    def exchange(g, b):
        part = pl.ds(g * per_part, per_part)
        return pltpu.make_async_remote_copy(
            sum_send.at[b, part], sum_recv.at[b, part], ss_sem.at[b, g], sr_sem.at[b, g],
            device_id={"seq": partner_of[b]}, device_id_type=MESH,
        )

    exchange_total(0).start()
    loads[0].wait()
    loads[1].wait()
    loads[2].start()
    loads[3].start()

    nothing = jnp.zeros((width, width), BF16)
    for g in range(PARTS):
        members = range(g * per_part, (g + 1) * per_part)

        @pl.loop(0, quads)
        def _(c):
            rows = quad_rows(c)
            decay = jnp.exp(tots[c][0:1, :] - cum[rows, :])
            for h in members:
                hs = head_cols(h)
                scaled = (k[rows, hs].astype(F32) * decay[:, h : h + 1]).astype(BF16)
                state[c, h] = lax.dot_general(
                    scaled, v[rows, hs], (((0,), (0,)), ((), ())), preferred_element_type=F32
                )

        for h in members:
            s0, s2 = state[0, h], state[2, h]
            low = e1[:, h : h + 1] * s0 + state[1, h]
            whole = e23[:, h : h + 1] * low + e3[:, h : h + 1] * s2 + state[3, h]
            summary[h] = whole
            sum_send[0, h] = whole.astype(BF16)
            low_b = low.astype(BF16)
            lev[0, h, :, :width] = nothing
            lev[0, h, :, width:] = nothing
            lev[1, h, :, :width] = s0.astype(BF16)
            lev[1, h, :, width:] = nothing
            lev[2, h, :, :width] = nothing
            lev[2, h, :, width:] = low_b
            lev[3, h, :, :width] = s2.astype(BF16)
            lev[3, h, :, width:] = low_b
        exchange(g, 0).start()

    loads[2].wait()

    def local_quad(c, members):
        rows = quad_rows(c)
        cq = cum[rows, :]
        ecq = jnp.exp(cq)
        ct = cumt[c]
        lwq = lw_ref[rows, :]
        is_last = (c == quads - 1).astype(F32)
        g4 = is_last * jnp.exp(t[2]) + (1.0 - is_last)
        causal = row_id >= col_id
        same = (row_id // SPAN) == (col_id // SPAN)
        near = (row_id // (2 * SPAN)) == (col_id // (2 * SPAN))
        for h in members:
            hs = head_cols(h)
            at = h * levels
            qh = q[rows, hs]
            s = lax.dot_general(
                qh, k[rows, hs], (((1,), (1,)), ((), ())), preferred_element_type=F32
            )
            spread = jnp.where(causal, cq[:, h : h + 1] - ct[h : h + 1, :], -1e30)
            weight = jnp.where(
                same,
                lwq[:, at : at + 1],
                jnp.where(near, lwq[:, at + 1 : at + 2], lwq[:, at + 2 : at + 3]),
            )
            probs = (s * jnp.exp(spread) * weight).astype(BF16)
            o = jnp.dot(probs, v[rows, hs], preferred_element_type=F32)
            read = jnp.dot(qh, lev[c, h], preferred_element_type=F32)
            col = ecq[:, h : h + 1]
            o = o + (col * lwq[:, at + 3 : at + 4]) * read[:, :width]
            o = o + (col * lwq[:, at + 4 : at + 5] * g4[:, h : h + 1]) * read[:, width:]
            attn[rows, hs] = o

    far_gain, mine_by, other_by = [], [], []
    offset = jnp.zeros_like(total)
    turns = PARTS + bits - 1
    units = [(g, half) for g in range(PARTS) for half in range(2)]
    for turn in range(turns):
        for g, half in units[turn * len(units) // turns : (turn + 1) * len(units) // turns]:

            @pl.loop(half * quads // 2, (half + 1) * quads // 2)
            def _(c):
                local_quad(c, range(g * per_part, (g + 1) * per_part))

        for b in range(bits):
            g = turn - b
            if g < 0 or g >= PARTS:
                continue
            if g == 0:
                exchange_total(b).wait()
                flag = bit_of[b].astype(F32)
                other = tot_recv[b][0:1, :]
                far_gain.append(flag * jnp.exp(offset))
                mine_by.append(flag + (1.0 - flag) * jnp.exp(other))
                other_by.append(flag * jnp.exp(total) + (1.0 - flag))
                offset = offset + flag * other
                total = total + other
                if b < bits - 1:
                    tot_send[b + 1] = jnp.broadcast_to(total, (8, 128))
                    exchange_total(b + 1).start()
            exchange(g, b).wait()
            for h in range(g * per_part, (g + 1) * per_part):
                got = sum_recv[b, h]
                if b < bits - 1:
                    joint = (
                        mine_by[b][:, h : h + 1] * summary[h]
                        + other_by[b][:, h : h + 1] * got.astype(F32)
                    )
                    summary[h] = joint
                    sum_send[b + 1, h] = joint.astype(BF16)
                far[h, :, b * width : (b + 1) * width] = got
            if b < bits - 1:
                exchange(g, b + 1).start()

    loads[3].wait()

    def finish_quad(c, at_row):
        rows = quad_rows(c)
        ecq = jnp.exp(cum[rows, :])
        lwq = lw_ref[rows, :]
        lead = jnp.zeros_like(before[0])
        for n in range(1, quads):
            lead = lead + (c == n).astype(F32) * before[n]
        lead = jnp.exp(lead)
        for h in range(heads):
            hs = head_cols(h)
            read = jnp.dot(q[rows, hs], far[h], preferred_element_type=F32)
            o = attn[rows, hs]
            col = ecq[:, h : h + 1]
            for b in range(bits):
                at = h * levels + 5 + b
                gain = (lead * far_gain[b])[:, h : h + 1]
                o = o + (col * lwq[:, at : at + 1] * gain) * read[:, b * width : (b + 1) * width]
            mean_square = jnp.mean(o * o, axis=-1, keepdims=True)
            o = o * lax.rsqrt(mean_square + 1e-6) * gain_ref[h : h + 1, :]
            normed[pl.ds(pl.multiple_of(at_row, QUAD), QUAD), hs] = o.astype(BF16)

    def to_core(i, j):
        return pltpu.make_async_remote_copy(
            core_send.at[i, j], core_recv.at[i, j], cs_sem.at[i, j], cr_sem.at[i, j],
            device_id={"head": other_core}, device_id_type=MESH,
        )

    def piece(j):
        return pl.ds(pl.multiple_of(j * piece_cols, piece_cols), piece_cols)

    def to_chip(i, j):
        return pltpu.make_async_remote_copy(
            x_send.at[i, j], x_recv.at[i, :, piece(j)], xs_sem.at[i, j], xr_sem.at[i, j],
            device_id={"head": chip_of[i] * 2 + core}, device_id_type=MESH,
        )

    def to_out(j):
        return pltpu.make_async_copy(acc.at[j], out_ref.at[:, piece(j)], out_sem.at[j])

    def product(which, j):
        rows = pl.ds(pl.multiple_of(which * block, block), block)
        return jnp.dot(normed[rows, :], w[:, piece(j)], preferred_element_type=F32)

    per_group = group // QUAD
    for i in range(chips):

        @pl.loop(0, per_group)
        def _(n):
            finish_quad(chip_of[i] * per_group + n, n * QUAD)

        @pl.loop(0, PIECES + 1)
        def _(j):
            @pl.when(j < PIECES)
            def _():
                core_send[i, j] = product(1 - core, j).astype(BF16)
                to_core(i, j).start()

            @pl.when(j > 0)
            def _():
                mine = product(core, j - 1)
                to_core(i, j - 1).wait()
                mine = mine + core_recv[i, j - 1].astype(F32)
                if i < chips - 1:
                    x_send[i, j - 1] = mine.astype(BF16)
                    to_chip(i, j - 1).start()
                else:
                    acc[j - 1] = mine
                    to_out(j - 1).start()

    @pl.loop(0, PIECES)
    def _(j):
        to_out(j).wait()
        for i in range(chips - 1):
            to_chip(i, j).wait()


def body(chips, bits, queries, keys, values, log_decay, level_weight, norm_gain, out_weight):
    rows, heads, width = queries.shape
    levels = level_weight.shape[2]
    depth, columns = out_weight.shape
    block = rows // (2 * chips)
    quads = rows // QUAD
    flat = (rows, heads * width)
    piece = (PIECES, block, columns // PIECES)
    decay = jnp.transpose(log_decay)
    weights = jnp.transpose(level_weight, (1, 2, 0)).reshape(heads * levels, rows)
    vmem = pl.BlockSpec(memory_space=pltpu.VMEM)
    hbm = pl.BlockSpec(memory_space=pl.ANY)
    dma = pltpu.SemaphoreType.DMA
    mine, others = pl.pallas_call(
        functools.partial(kernel, chips, bits, heads, levels, width),
        out_shape=(
            jax.ShapeDtypeStruct((block, columns), F32),
            jax.ShapeDtypeStruct((chips - 1, block, columns), BF16),
        ),
        in_specs=[hbm] * 4 + [vmem] * 3,
        out_specs=(hbm, hbm),
        scratch_shapes=[
            pltpu.VMEM(flat, BF16),
            pltpu.VMEM(flat, BF16),
            pltpu.VMEM(flat, BF16),
            pltpu.VMEM((depth, columns), BF16),
            pltpu.VMEM((rows, 128), F32),
            pltpu.VMEM((quads, heads, QUAD), F32),
            pltpu.VMEM((rows, heads * levels), F32),
            pltpu.VMEM((quads, 8, 128), F32),
            pltpu.VMEM((quads, heads, width, width), F32),
            pltpu.VMEM((quads, heads, width, 2 * width), BF16),
            pltpu.VMEM(flat, F32),
            pltpu.VMEM((2 * block, heads * width), BF16),
            pltpu.VMEM((heads, width, width), F32),
            pltpu.VMEM((bits, heads, width, width), BF16),
            pltpu.VMEM((bits, heads, width, width), BF16),
            pltpu.VMEM((bits, 8, 128), F32),
            pltpu.VMEM((bits, 8, 128), F32),
            pltpu.VMEM((heads, width, bits * width), BF16),
            pltpu.VMEM((chips,) + piece, BF16),
            pltpu.VMEM((chips,) + piece, BF16),
            pltpu.VMEM((chips - 1,) + piece, BF16),
            pltpu.VMEM(piece, F32),
            dma((4,)),
            dma((bits, PARTS)),
            dma((bits, PARTS)),
            dma((bits,)),
            dma((bits,)),
            dma((chips, PIECES)),
            dma((chips, PIECES)),
            dma((chips - 1, PIECES)),
            dma((chips - 1, PIECES)),
            dma((PIECES,)),
        ],
        compiler_params=pltpu.CompilerParams(
            collective_id=0, has_side_effects=True, vmem_limit_bytes=58 * 1024 * 1024
        ),
    )(
        queries.reshape(flat),
        keys.reshape(flat),
        values.reshape(flat),
        out_weight,
        decay,
        weights,
        norm_gain,
    )
    for i in range(chips - 1):
        mine = mine + others[i].astype(F32)
    return mine.astype(BF16)


def solution(mesh):
    chips = mesh.shape["head"] // 2
    bits = mesh.shape["seq"].bit_length() - 1
    return jax.shard_map(
        functools.partial(body, chips, bits),
        mesh=mesh,
        in_specs=(
            P("seq", "head", None),
            P("seq", "head", None),
            P("seq", "head", None),
            P("seq", "head"),
            P("seq", "head", None),
            P("head", None),
            P("head", None),
        ),
        out_specs=P(("seq", "head"), None),
        check_vma=False,
    )
```

```python
import functools

import jax
import jax.numpy as jnp
from jax import lax
from jax.experimental import pallas as pl
from jax.experimental.pallas import tpu as pltpu
from jax.sharding import PartitionSpec as P

SPAN = 64
QUAD = 4 * SPAN
PIECES = 4
PARTS = 4
F32 = jnp.float32
BF16 = jnp.bfloat16
HIGH = lax.Precision.HIGHEST
MESH = pl.DeviceIdType.MESH


def kernel(
    chips, bits, heads, levels, width,
    q_hbm, k_hbm, v_hbm, w_hbm, ldt_ref, lwt_ref, gain_ref, out_ref, x_recv,
    q, k, v, w, cum, cumt, lw_ref, tots, state, lev, attn, normed,
    summary, sum_send, sum_recv, tot_send, tot_recv, far,
    core_send, core_recv, x_send, acc,
    in_sem, ss_sem, sr_sem, ts_sem, tr_sem, cs_sem, cr_sem, xs_sem, xr_sem, out_sem,
):
    rows_all = q.shape[0]
    quads = rows_all // QUAD
    block = out_ref.shape[0]
    group = 2 * block
    piece_cols = out_ref.shape[1] // PIECES
    per_part = heads // PARTS
    position = lax.axis_index("seq")
    head_id = lax.axis_index("head")
    chip = head_id // 2
    core = head_id % 2
    other_core = chip * 2 + (1 - core)

    loads = [
        pltpu.make_async_copy(src, dst, in_sem.at[n])
        for n, (src, dst) in enumerate(((k_hbm, k), (v_hbm, v), (q_hbm, q), (w_hbm, w)))
    ]
    loads[0].start()
    loads[1].start()

    bit_of = [(position // (1 << b)) % 2 for b in range(bits)]
    partner_of = [position + (1 - 2 * bit_of[b]) * (1 << b) for b in range(bits)]
    chip_of = [(chip + 1 + i) % chips for i in range(chips)]

    barrier = pltpu.get_barrier_semaphore()
    for b in range(bits):
        pl.semaphore_signal(barrier, inc=1, device_id={"seq": partner_of[b]}, device_id_type=MESH)
    pl.semaphore_signal(barrier, inc=1, device_id={"head": other_core}, device_id_type=MESH)
    for i in range(chips - 1):
        pl.semaphore_signal(
            barrier, inc=1, device_id={"head": chip_of[i] * 2 + core}, device_id_type=MESH
        )
    pl.semaphore_wait(barrier, bits + chips)

    row_id = lax.broadcasted_iota(jnp.int32, (QUAD, QUAD), 0)
    col_id = lax.broadcasted_iota(jnp.int32, (QUAD, QUAD), 1)

    def head_cols(h):
        return slice(h * width, (h + 1) * width)

    def quad_rows(c):
        return pl.ds(pl.multiple_of(c * QUAD, QUAD), QUAD)

    def lane_head(ids):
        return sum((ids >= h * levels).astype(jnp.int32) for h in range(1, heads))

    def lane(h):
        return slice(h * levels, h * levels + 1)

    lane_id = lax.broadcasted_iota(jnp.int32, (1, 128), 1)
    level_id = lane_id - levels * lane_head(lane_id)
    spread_head = lane_head(lax.broadcasted_iota(jnp.int32, (128, heads), 0))
    spread = (spread_head == lax.broadcasted_iota(jnp.int32, (128, heads), 1)).astype(F32)

    @pl.loop(0, quads)
    def _(c):
        rows = quad_rows(c)
        lower = (row_id >= col_id).astype(F32)
        upper = (row_id <= col_id).astype(F32)
        decay = ldt_ref[:, rows]
        cumt[c] = jnp.dot(decay, upper, precision=HIGH, preferred_element_type=F32)
        wide = jnp.dot(spread, decay, precision=HIGH, preferred_element_type=F32)
        cq = lax.dot_general(
            lower, wide, (((1,), (1,)), ((), ())), precision=HIGH, preferred_element_type=F32
        )
        cum[rows, :] = cq
        tots[c] = jnp.broadcast_to(cq[QUAD - 1 : QUAD, :], (8, 128))
        padding = jnp.zeros((128 - heads * levels, QUAD), F32)
        weights = jnp.transpose(jnp.concatenate([lwt_ref[:, rows], padding], axis=0))
        lw_ref[rows, :] = weights * jnp.where(level_id >= 3, jnp.exp(cq), 1.0)

    t = [tots[c][0:1, :] for c in range(quads)]
    e1, e3, e23 = jnp.exp(t[1]), jnp.exp(t[3]), jnp.exp(t[2] + t[3])
    total = t[0] + t[1] + t[2] + t[3]
    before = [jnp.zeros_like(total), t[0], t[0] + t[1], t[0] + t[1] + t[2]]
    tot_send[0] = jnp.broadcast_to(total, (8, 128))

    def exchange_total(b):
        return pltpu.make_async_remote_copy(
            tot_send.at[b], tot_recv.at[b], ts_sem.at[b], tr_sem.at[b],
            device_id={"seq": partner_of[b]}, device_id_type=MESH,
        )

    def exchange(g, b):
        part = pl.ds(g * per_part, per_part)
        return pltpu.make_async_remote_copy(
            sum_send.at[b, part], sum_recv.at[b, part], ss_sem.at[b, g], sr_sem.at[b, g],
            device_id={"seq": partner_of[b]}, device_id_type=MESH,
        )

    exchange_total(0).start()
    loads[0].wait()
    loads[1].wait()
    loads[2].start()
    loads[3].start()

    nothing = jnp.zeros((width, width), BF16)
    for g in range(PARTS):
        members = range(g * per_part, (g + 1) * per_part)

        @pl.loop(0, quads)
        def _(c):
            rows = quad_rows(c)
            decay = jnp.exp(tots[c][0:1, :] - cum[rows, :])
            for h in members:
                hs = head_cols(h)
                scaled = (k[rows, hs].astype(F32) * decay[:, lane(h)]).astype(BF16)
                state[c, h] = lax.dot_general(
                    scaled, v[rows, hs], (((0,), (0,)), ((), ())), preferred_element_type=F32
                )

        for h in members:
            s0, s2 = state[0, h], state[2, h]
            low = e1[:, lane(h)] * s0 + state[1, h]
            whole = e23[:, lane(h)] * low + e3[:, lane(h)] * s2 + state[3, h]
            summary[h] = whole
            sum_send[0, h] = whole.astype(BF16)
            low_b = low.astype(BF16)
            lev[0, h, :, :width] = nothing
            lev[0, h, :, width:] = nothing
            lev[1, h, :, :width] = s0.astype(BF16)
            lev[1, h, :, width:] = nothing
            lev[2, h, :, :width] = nothing
            lev[2, h, :, width:] = low_b
            lev[3, h, :, :width] = s2.astype(BF16)
            lev[3, h, :, width:] = low_b
        exchange(g, 0).start()

    loads[2].wait()

    strip_row = lax.broadcasted_iota(jnp.int32, (SPAN, 2 * SPAN), 0)
    strip_col = lax.broadcasted_iota(jnp.int32, (SPAN, 2 * SPAN), 1)

    def local_quad(c, members):
        base = c * QUAD
        ct = cumt[c]
        is_last = (c == quads - 1).astype(F32)
        g4 = jnp.where(level_id == 4, is_last * jnp.exp(t[2]) + (1.0 - is_last), 1.0)
        for side in range(2):
            rows = pl.ds(pl.multiple_of(base + side * 2 * SPAN, 2 * SPAN), 2 * SPAN)
            seen = pl.ds(pl.multiple_of(base, QUAD), (side + 1) * 2 * SPAN)
            cq = cum[rows, :]
            fq = lw_ref[rows, :] * g4
            for h in members:
                hs = head_cols(h)
                at = h * levels
                qh = q[rows, hs]
                s = lax.dot_general(
                    qh, k[seen, hs], (((1,), (1,)), ((), ())), preferred_element_type=F32
                )
                strips = []
                for n in range(2):
                    top = slice(n * SPAN, (n + 1) * SPAN)
                    col = cq[top, lane(h)]
                    own = fq[top, at : at + 1]
                    if n == 1:
                        own = jnp.where(strip_col < SPAN, fq[top, at + 1 : at + 2], own)
                    diag = slice(side * 2 * SPAN, (side + 1) * 2 * SPAN)
                    gap = jnp.where(
                        strip_row + n * SPAN >= strip_col, col - ct[h : h + 1, diag], -1e30
                    )
                    strip = (s[top, diag] * (jnp.exp(gap) * own)).astype(BF16)
                    if side == 1:
                        gap = col - ct[h : h + 1, : 2 * SPAN]
                        far_side = s[top, : 2 * SPAN] * (jnp.exp(gap) * fq[top, at + 2 : at + 3])
                        strip = jnp.concatenate([far_side.astype(BF16), strip], axis=1)
                    strips.append(strip)
                probs = jnp.concatenate(strips, axis=0)
                o = jnp.dot(probs, v[seen, hs], preferred_element_type=F32)
                read = jnp.dot(qh, lev[c, h], preferred_element_type=F32)
                o = o + fq[:, at + 3 : at + 4] * read[:, :width]
                o = o + fq[:, at + 4 : at + 5] * read[:, width:]
                attn[rows, hs] = o

    far_gain, mine_by, other_by = [], [], []
    offset = jnp.zeros_like(total)
    turns = PARTS + bits - 1
    units = [(g, half) for g in range(PARTS) for half in range(2)]
    for turn in range(turns):
        for g, half in units[turn * len(units) // turns : (turn + 1) * len(units) // turns]:

            @pl.loop(half * quads // 2, (half + 1) * quads // 2)
            def _(c):
                local_quad(c, range(g * per_part, (g + 1) * per_part))

        for b in range(bits):
            g = turn - b
            if g < 0 or g >= PARTS:
                continue
            if g == 0:
                exchange_total(b).wait()
                flag = bit_of[b].astype(F32)
                other = tot_recv[b][0:1, :]
                far_gain.append(flag * jnp.exp(offset))
                mine_by.append(flag + (1.0 - flag) * jnp.exp(other))
                other_by.append(flag * jnp.exp(total) + (1.0 - flag))
                offset = offset + flag * other
                total = total + other
                if b < bits - 1:
                    tot_send[b + 1] = jnp.broadcast_to(total, (8, 128))
                    exchange_total(b + 1).start()
            exchange(g, b).wait()
            for h in range(g * per_part, (g + 1) * per_part):
                got = sum_recv[b, h]
                if b < bits - 1:
                    joint = (
                        mine_by[b][:, lane(h)] * summary[h]
                        + other_by[b][:, lane(h)] * got.astype(F32)
                    )
                    summary[h] = joint
                    sum_send[b + 1, h] = joint.astype(BF16)
                far[h, :, b * width : (b + 1) * width] = got
            if b < bits - 1:
                exchange(g, b + 1).start()

    loads[3].wait()

    reach = jnp.ones((1, 128), F32)
    for b in range(bits):
        reach = jnp.where(level_id == 5 + b, far_gain[b], reach)

    def finish_quad(c, at_row):
        lead = jnp.zeros_like(before[0])
        for n in range(1, quads):
            lead = lead + (c == n).astype(F32) * before[n]
        gain = reach * jnp.exp(lead)
        for side in range(2):
            skip = side * 2 * SPAN
            rows = pl.ds(pl.multiple_of(c * QUAD + skip, 2 * SPAN), 2 * SPAN)
            into = pl.ds(pl.multiple_of(at_row + skip, 2 * SPAN), 2 * SPAN)
            fq = lw_ref[rows, :] * gain
            for h in range(heads):
                hs = head_cols(h)
                read = jnp.dot(q[rows, hs], far[h], preferred_element_type=F32)
                o = attn[rows, hs]
                for b in range(bits):
                    at = h * levels + 5 + b
                    o = o + fq[:, at : at + 1] * read[:, b * width : (b + 1) * width]
                mean_square = jnp.mean(o * o, axis=-1, keepdims=True)
                o = o * lax.rsqrt(mean_square + 1e-6) * gain_ref[h : h + 1, :]
                normed[into, hs] = o.astype(BF16)

    def to_core(i, j):
        return pltpu.make_async_remote_copy(
            core_send.at[i, j], core_recv.at[i, j], cs_sem.at[i, j], cr_sem.at[i, j],
            device_id={"head": other_core}, device_id_type=MESH,
        )

    def piece(j):
        return pl.ds(pl.multiple_of(j * piece_cols, piece_cols), piece_cols)

    def to_chip(i, j):
        return pltpu.make_async_remote_copy(
            x_send.at[i, j], x_recv.at[i, :, piece(j)], xs_sem.at[i, j], xr_sem.at[i, j],
            device_id={"head": chip_of[i] * 2 + core}, device_id_type=MESH,
        )

    def to_out(j):
        return pltpu.make_async_copy(acc.at[j], out_ref.at[:, piece(j)], out_sem.at[j])

    def product(which, j):
        rows = pl.ds(pl.multiple_of(which * block, block), block)
        return jnp.dot(normed[rows, :], w[:, piece(j)], preferred_element_type=F32)

    per_group = group // QUAD
    for i in range(chips):

        @pl.loop(0, per_group)
        def _(n):
            finish_quad(chip_of[i] * per_group + n, n * QUAD)

        @pl.loop(0, PIECES + 1)
        def _(j):
            @pl.when(j < PIECES)
            def _():
                core_send[i, j] = product(1 - core, j).astype(BF16)
                to_core(i, j).start()

            @pl.when(j > 0)
            def _():
                mine = product(core, j - 1)
                to_core(i, j - 1).wait()
                mine = mine + core_recv[i, j - 1].astype(F32)
                if i < chips - 1:
                    x_send[i, j - 1] = mine.astype(BF16)
                    to_chip(i, j - 1).start()
                else:
                    acc[j - 1] = mine.astype(BF16)
                    to_out(j - 1).start()

    @pl.loop(0, PIECES)
    def _(j):
        to_out(j).wait()
        for i in range(chips - 1):
            to_chip(i, j).wait()


def body(chips, bits, queries, keys, values, log_decay, level_weight, norm_gain, out_weight):
    rows, heads, width = queries.shape
    levels = level_weight.shape[2]
    depth, columns = out_weight.shape
    block = rows // (2 * chips)
    quads = rows // QUAD
    flat = (rows, heads * width)
    piece = (PIECES, block, columns // PIECES)
    decay = jnp.transpose(log_decay)
    weights = jnp.transpose(level_weight, (1, 2, 0)).reshape(heads * levels, rows)
    vmem = pl.BlockSpec(memory_space=pltpu.VMEM)
    hbm = pl.BlockSpec(memory_space=pl.ANY)
    dma = pltpu.SemaphoreType.DMA
    mine, others = pl.pallas_call(
        functools.partial(kernel, chips, bits, heads, levels, width),
        out_shape=(
            jax.ShapeDtypeStruct((block, columns), BF16),
            jax.ShapeDtypeStruct((chips - 1, block, columns), BF16),
        ),
        in_specs=[hbm] * 4 + [vmem] * 3,
        out_specs=(hbm, hbm),
        scratch_shapes=[
            pltpu.VMEM(flat, BF16),
            pltpu.VMEM(flat, BF16),
            pltpu.VMEM(flat, BF16),
            pltpu.VMEM((depth, columns), BF16),
            pltpu.VMEM((rows, 128), F32),
            pltpu.VMEM((quads, heads, QUAD), F32),
            pltpu.VMEM((rows, 128), F32),
            pltpu.VMEM((quads, 8, 128), F32),
            pltpu.VMEM((quads, heads, width, width), F32),
            pltpu.VMEM((quads, heads, width, 2 * width), BF16),
            pltpu.VMEM(flat, F32),
            pltpu.VMEM((2 * block, heads * width), BF16),
            pltpu.VMEM((heads, width, width), F32),
            pltpu.VMEM((bits, heads, width, width), BF16),
            pltpu.VMEM((bits, heads, width, width), BF16),
            pltpu.VMEM((bits, 8, 128), F32),
            pltpu.VMEM((bits, 8, 128), F32),
            pltpu.VMEM((heads, width, bits * width), BF16),
            pltpu.VMEM((chips,) + piece, BF16),
            pltpu.VMEM((chips,) + piece, BF16),
            pltpu.VMEM((chips - 1,) + piece, BF16),
            pltpu.VMEM(piece, BF16),
            dma((4,)),
            dma((bits, PARTS)),
            dma((bits, PARTS)),
            dma((bits,)),
            dma((bits,)),
            dma((chips, PIECES)),
            dma((chips, PIECES)),
            dma((chips - 1, PIECES)),
            dma((chips - 1, PIECES)),
            dma((PIECES,)),
        ],
        compiler_params=pltpu.CompilerParams(
            collective_id=0, has_side_effects=True, vmem_limit_bytes=58 * 1024 * 1024
        ),
    )(
        queries.reshape(flat),
        keys.reshape(flat),
        values.reshape(flat),
        out_weight,
        decay,
        weights,
        norm_gain,
    )
    mine = mine.astype(F32)
    for i in range(chips - 1):
        mine = mine + others[i].astype(F32)
    return mine.astype(BF16)


def solution(mesh):
    chips = mesh.shape["head"] // 2
    bits = mesh.shape["seq"].bit_length() - 1
    return jax.shard_map(
        functools.partial(body, chips, bits),
        mesh=mesh,
        in_specs=(
            P("seq", "head", None),
            P("seq", "head", None),
            P("seq", "head", None),
            P("seq", "head"),
            P("seq", "head", None),
            P("head", None),
            P("head", None),
        ),
        out_specs=P(("seq", "head"), None),
        check_vma=False,
    )
```

```python
import functools

import jax
import jax.numpy as jnp
from jax import lax
from jax.experimental import pallas as pl
from jax.experimental.pallas import tpu as pltpu
from jax.sharding import PartitionSpec as P

SPAN = 64
QUAD = 4 * SPAN
PIECES = 4
PARTS = 4
F32 = jnp.float32
BF16 = jnp.bfloat16
HIGH = lax.Precision.HIGHEST
MESH = pl.DeviceIdType.MESH


def kernel(
    chips, bits, heads, levels, width,
    q_hbm, k_hbm, v_hbm, w_hbm, ldt_ref, lwt_ref, gain_ref, out_ref, x_recv,
    q, k, v, w, cum, cumt, lw_ref, tots, state, lev, attn, normed,
    summary, sum_send, sum_recv, tot_send, tot_recv, far,
    core_send, core_recv, x_send, acc,
    in_sem, ss_sem, sr_sem, ts_sem, tr_sem, cs_sem, cr_sem, xs_sem, xr_sem, out_sem,
):
    rows_all = q.shape[0]
    quads = rows_all // QUAD
    block = out_ref.shape[0]
    group = 2 * block
    piece_cols = out_ref.shape[1] // PIECES
    per_part = heads // PARTS
    position = lax.axis_index("seq")
    head_id = lax.axis_index("head")
    chip = head_id // 2
    core = head_id % 2
    other_core = chip * 2 + (1 - core)

    loads = [
        pltpu.make_async_copy(src, dst, in_sem.at[n])
        for n, (src, dst) in enumerate(((k_hbm, k), (v_hbm, v), (q_hbm, q), (w_hbm, w)))
    ]
    loads[0].start()
    loads[1].start()

    bit_of = [(position // (1 << b)) % 2 for b in range(bits)]
    partner_of = [position + (1 - 2 * bit_of[b]) * (1 << b) for b in range(bits - 1)]
    row = 1 << (bits // 2)
    half = 1 << (bits - 1)
    gives = (position >= half - row) & (position < 2 * half - row)
    takes = position >= half
    above = (position + row) % (2 * half)
    below = (position - row + 2 * half) % (2 * half)
    chip_of = [(chip + 1 + i) % chips for i in range(chips)]

    barrier = pltpu.get_barrier_semaphore()
    for b in range(bits - 1):
        pl.semaphore_signal(barrier, inc=1, device_id={"seq": partner_of[b]}, device_id_type=MESH)

    @pl.when(gives)
    def _():
        pl.semaphore_signal(barrier, inc=1, device_id={"seq": above}, device_id_type=MESH)

    @pl.when(takes)
    def _():
        pl.semaphore_signal(barrier, inc=1, device_id={"seq": below}, device_id_type=MESH)

    pl.semaphore_signal(barrier, inc=1, device_id={"head": other_core}, device_id_type=MESH)
    for i in range(chips - 1):
        pl.semaphore_signal(
            barrier, inc=1, device_id={"head": chip_of[i] * 2 + core}, device_id_type=MESH
        )
    chained = position // half + ((position + row) // half) % 2
    pl.semaphore_wait(barrier, bits - 1 + chips + chained)

    row_id = lax.broadcasted_iota(jnp.int32, (QUAD, QUAD), 0)
    col_id = lax.broadcasted_iota(jnp.int32, (QUAD, QUAD), 1)

    def head_cols(h):
        return slice(h * width, (h + 1) * width)

    def quad_rows(c):
        return pl.ds(pl.multiple_of(c * QUAD, QUAD), QUAD)

    def lane_head(ids):
        return sum((ids >= h * levels).astype(jnp.int32) for h in range(1, heads))

    def lane(h):
        return slice(h * levels, h * levels + 1)

    lane_id = lax.broadcasted_iota(jnp.int32, (1, 128), 1)
    level_id = lane_id - levels * lane_head(lane_id)
    spread_head = lane_head(lax.broadcasted_iota(jnp.int32, (128, heads), 0))
    spread = (spread_head == lax.broadcasted_iota(jnp.int32, (128, heads), 1)).astype(F32)

    @pl.loop(0, quads)
    def _(c):
        rows = quad_rows(c)
        lower = (row_id >= col_id).astype(F32)
        upper = (row_id <= col_id).astype(F32)
        decay = ldt_ref[:, rows]
        cumt[c] = jnp.dot(decay, upper, precision=HIGH, preferred_element_type=F32)
        wide = jnp.dot(spread, decay, precision=HIGH, preferred_element_type=F32)
        cq = lax.dot_general(
            lower, wide, (((1,), (1,)), ((), ())), precision=HIGH, preferred_element_type=F32
        )
        cum[rows, :] = cq
        tots[c] = jnp.broadcast_to(cq[QUAD - 1 : QUAD, :], (8, 128))
        padding = jnp.zeros((128 - heads * levels, QUAD), F32)
        weights = jnp.transpose(jnp.concatenate([lwt_ref[:, rows], padding], axis=0))
        lw_ref[rows, :] = weights * jnp.where(level_id >= 3, jnp.exp(cq), 1.0)

    t = [tots[c][0:1, :] for c in range(quads)]
    e1, e3, e23 = jnp.exp(t[1]), jnp.exp(t[3]), jnp.exp(t[2] + t[3])
    total = t[0] + t[1] + t[2] + t[3]
    before = [jnp.zeros_like(total), t[0], t[0] + t[1], t[0] + t[1] + t[2]]
    tot_send[0] = jnp.broadcast_to(total, (8, 128))

    def exchange_total(b):
        return pltpu.make_async_remote_copy(
            tot_send.at[b], tot_recv.at[b], ts_sem.at[b], tr_sem.at[b],
            device_id={"seq": partner_of[b]}, device_id_type=MESH,
        )

    def exchange(g, b):
        part = pl.ds(g * per_part, per_part)
        return pltpu.make_async_remote_copy(
            sum_send.at[b, part], sum_recv.at[b, part], ss_sem.at[b, g], sr_sem.at[b, g],
            device_id={"seq": partner_of[b]}, device_id_type=MESH,
        )

    def hand_on(g, src):
        part = pl.ds(g * per_part, per_part)
        b = bits - 1
        return pltpu.make_async_remote_copy(
            src.at[b, part], sum_recv.at[b, part], ss_sem.at[b, g], sr_sem.at[b, g],
            device_id={"seq": above}, device_id_type=MESH,
        )

    exchange_total(0).start()
    loads[0].wait()
    loads[1].wait()
    loads[2].start()
    loads[3].start()

    nothing = jnp.zeros((width, width), BF16)
    for g in range(PARTS):
        members = range(g * per_part, (g + 1) * per_part)

        @pl.loop(0, quads)
        def _(c):
            rows = quad_rows(c)
            decay = jnp.exp(tots[c][0:1, :] - cum[rows, :])
            for h in members:
                hs = head_cols(h)
                scaled = (k[rows, hs].astype(F32) * decay[:, lane(h)]).astype(BF16)
                state[c, h] = lax.dot_general(
                    scaled, v[rows, hs], (((0,), (0,)), ((), ())), preferred_element_type=F32
                )

        for h in members:
            s0, s2 = state[0, h], state[2, h]
            low = e1[:, lane(h)] * s0 + state[1, h]
            whole = e23[:, lane(h)] * low + e3[:, lane(h)] * s2 + state[3, h]
            summary[h] = whole
            sum_send[0, h] = whole.astype(BF16)
            low_b = low.astype(BF16)
            lev[0, h, :, :width] = nothing
            lev[0, h, :, width:] = nothing
            lev[1, h, :, :width] = s0.astype(BF16)
            lev[1, h, :, width:] = nothing
            lev[2, h, :, :width] = nothing
            lev[2, h, :, width:] = low_b
            lev[3, h, :, :width] = s2.astype(BF16)
            lev[3, h, :, width:] = low_b
        exchange(g, 0).start()

    loads[2].wait()

    strip_row = lax.broadcasted_iota(jnp.int32, (SPAN, 2 * SPAN), 0)
    strip_col = lax.broadcasted_iota(jnp.int32, (SPAN, 2 * SPAN), 1)

    def local_quad(c, members):
        base = c * QUAD
        ct = cumt[c]
        is_last = (c == quads - 1).astype(F32)
        g4 = jnp.where(level_id == 4, is_last * jnp.exp(t[2]) + (1.0 - is_last), 1.0)
        for side in range(2):
            rows = pl.ds(pl.multiple_of(base + side * 2 * SPAN, 2 * SPAN), 2 * SPAN)
            seen = pl.ds(pl.multiple_of(base, QUAD), (side + 1) * 2 * SPAN)
            cq = cum[rows, :]
            fq = lw_ref[rows, :] * g4
            for h in members:
                hs = head_cols(h)
                at = h * levels
                qh = q[rows, hs]
                s = lax.dot_general(
                    qh, k[seen, hs], (((1,), (1,)), ((), ())), preferred_element_type=F32
                )
                strips = []
                for n in range(2):
                    top = slice(n * SPAN, (n + 1) * SPAN)
                    col = cq[top, lane(h)]
                    own = fq[top, at : at + 1]
                    if n == 1:
                        own = jnp.where(strip_col < SPAN, fq[top, at + 1 : at + 2], own)
                    diag = slice(side * 2 * SPAN, (side + 1) * 2 * SPAN)
                    gap = jnp.where(
                        strip_row + n * SPAN >= strip_col, col - ct[h : h + 1, diag], -1e30
                    )
                    strip = (s[top, diag] * (jnp.exp(gap) * own)).astype(BF16)
                    if side == 1:
                        gap = col - ct[h : h + 1, : 2 * SPAN]
                        far_side = s[top, : 2 * SPAN] * (jnp.exp(gap) * fq[top, at + 2 : at + 3])
                        strip = jnp.concatenate([far_side.astype(BF16), strip], axis=1)
                    strips.append(strip)
                probs = jnp.concatenate(strips, axis=0)
                o = jnp.dot(probs, v[seen, hs], preferred_element_type=F32)
                read = jnp.dot(qh, lev[c, h], preferred_element_type=F32)
                o = o + fq[:, at + 3 : at + 4] * read[:, :width]
                o = o + fq[:, at + 4 : at + 5] * read[:, width:]
                attn[rows, hs] = o

    far_gain, mine_by, other_by = [], [], []
    top = bits - 1
    offset = jnp.zeros_like(total)
    turns = PARTS + bits
    units = [(g, end) for g in range(PARTS) for end in range(2)]
    for turn in range(turns):
        for g, end in units[turn * len(units) // turns : (turn + 1) * len(units) // turns]:

            @pl.loop(end * quads // 2, (end + 1) * quads // 2)
            def _(c):
                local_quad(c, range(g * per_part, (g + 1) * per_part))

        for b in range(top):
            g = turn - b
            if g < 0 or g >= PARTS:
                continue
            if g == 0:
                exchange_total(b).wait()
                flag = bit_of[b].astype(F32)
                other = tot_recv[b][0:1, :]
                far_gain.append(flag * jnp.exp(offset))
                mine_by.append(flag + (1.0 - flag) * jnp.exp(other))
                other_by.append(flag * jnp.exp(total) + (1.0 - flag))
                offset = offset + flag * other
                total = total + other
                if b < top - 1:
                    tot_send[b + 1] = jnp.broadcast_to(total, (8, 128))
                    exchange_total(b + 1).start()
            exchange(g, b).wait()
            for h in range(g * per_part, (g + 1) * per_part):
                got = sum_recv[b, h]
                joint = (
                    mine_by[b][:, lane(h)] * summary[h]
                    + other_by[b][:, lane(h)] * got.astype(F32)
                )
                summary[h] = joint
                sum_send[b + 1, h] = joint.astype(BF16)
                far[h, :, b * width : (b + 1) * width] = got
            if b < top - 1:
                exchange(g, b + 1).start()
            else:

                @pl.when(gives & (position < half))
                def _():
                    hand_on(g, sum_send).start()

        g = turn - bits
        if g >= 0:

            @pl.when(takes)
            def _():
                hand_on(g, sum_recv).wait_recv()

            @pl.when(takes & gives)
            def _():
                hand_on(g, sum_recv).start()

            for h in range(g * per_part, (g + 1) * per_part):

                @pl.when(takes)
                def _():
                    far[h, :, top * width :] = sum_recv[top, h]

                @pl.when(position < half)
                def _():
                    far[h, :, top * width :] = nothing

    far_gain.append(bit_of[top].astype(F32) * jnp.exp(offset))

    @pl.when(gives)
    def _():
        for g in range(PARTS):
            hand_on(g, sum_send).wait_send()

    loads[3].wait()

    reach = jnp.ones((1, 128), F32)
    for b in range(bits):
        reach = jnp.where(level_id == 5 + b, far_gain[b], reach)

    def finish_quad(c, at_row):
        lead = jnp.zeros_like(before[0])
        for n in range(1, quads):
            lead = lead + (c == n).astype(F32) * before[n]
        gain = reach * jnp.exp(lead)
        for side in range(2):
            skip = side * 2 * SPAN
            rows = pl.ds(pl.multiple_of(c * QUAD + skip, 2 * SPAN), 2 * SPAN)
            into = pl.ds(pl.multiple_of(at_row + skip, 2 * SPAN), 2 * SPAN)
            fq = lw_ref[rows, :] * gain
            for h in range(heads):
                hs = head_cols(h)
                read = jnp.dot(q[rows, hs], far[h], preferred_element_type=F32)
                o = attn[rows, hs]
                for b in range(bits):
                    at = h * levels + 5 + b
                    o = o + fq[:, at : at + 1] * read[:, b * width : (b + 1) * width]
                mean_square = jnp.mean(o * o, axis=-1, keepdims=True)
                o = o * lax.rsqrt(mean_square + 1e-6) * gain_ref[h : h + 1, :]
                normed[into, hs] = o.astype(BF16)

    def to_core(i, j):
        return pltpu.make_async_remote_copy(
            core_send.at[i, j], core_recv.at[i, j], cs_sem.at[i, j], cr_sem.at[i, j],
            device_id={"head": other_core}, device_id_type=MESH,
        )

    def piece(j):
        return pl.ds(pl.multiple_of(j * piece_cols, piece_cols), piece_cols)

    def to_chip(i, j):
        return pltpu.make_async_remote_copy(
            x_send.at[i, j], x_recv.at[i, :, piece(j)], xs_sem.at[i, j], xr_sem.at[i, j],
            device_id={"head": chip_of[i] * 2 + core}, device_id_type=MESH,
        )

    def to_out(j):
        return pltpu.make_async_copy(acc.at[j], out_ref.at[:, piece(j)], out_sem.at[j])

    def product(which, j):
        rows = pl.ds(pl.multiple_of(which * block, block), block)
        return jnp.dot(normed[rows, :], w[:, piece(j)], preferred_element_type=F32)

    per_group = group // QUAD
    for i in range(chips):

        @pl.loop(0, per_group)
        def _(n):
            finish_quad(chip_of[i] * per_group + n, n * QUAD)

        @pl.loop(0, PIECES + 1)
        def _(j):
            @pl.when(j < PIECES)
            def _():
                core_send[i, j] = product(1 - core, j).astype(BF16)
                to_core(i, j).start()

            @pl.when(j > 0)
            def _():
                mine = product(core, j - 1)
                to_core(i, j - 1).wait()
                mine = mine + core_recv[i, j - 1].astype(F32)
                if i < chips - 1:
                    x_send[i, j - 1] = mine.astype(BF16)
                    to_chip(i, j - 1).start()
                else:
                    acc[j - 1] = mine.astype(BF16)
                    to_out(j - 1).start()

    @pl.loop(0, PIECES)
    def _(j):
        to_out(j).wait()
        for i in range(chips - 1):
            to_chip(i, j).wait()


def body(chips, bits, queries, keys, values, log_decay, level_weight, norm_gain, out_weight):
    rows, heads, width = queries.shape
    levels = level_weight.shape[2]
    depth, columns = out_weight.shape
    block = rows // (2 * chips)
    quads = rows // QUAD
    flat = (rows, heads * width)
    piece = (PIECES, block, columns // PIECES)
    decay = jnp.transpose(log_decay)
    weights = jnp.transpose(level_weight, (1, 2, 0)).reshape(heads * levels, rows)
    vmem = pl.BlockSpec(memory_space=pltpu.VMEM)
    hbm = pl.BlockSpec(memory_space=pl.ANY)
    dma = pltpu.SemaphoreType.DMA
    mine, others = pl.pallas_call(
        functools.partial(kernel, chips, bits, heads, levels, width),
        out_shape=(
            jax.ShapeDtypeStruct((block, columns), BF16),
            jax.ShapeDtypeStruct((chips - 1, block, columns), BF16),
        ),
        in_specs=[hbm] * 4 + [vmem] * 3,
        out_specs=(hbm, hbm),
        scratch_shapes=[
            pltpu.VMEM(flat, BF16),
            pltpu.VMEM(flat, BF16),
            pltpu.VMEM(flat, BF16),
            pltpu.VMEM((depth, columns), BF16),
            pltpu.VMEM((rows, 128), F32),
            pltpu.VMEM((quads, heads, QUAD), F32),
            pltpu.VMEM((rows, 128), F32),
            pltpu.VMEM((quads, 8, 128), F32),
            pltpu.VMEM((quads, heads, width, width), F32),
            pltpu.VMEM((quads, heads, width, 2 * width), BF16),
            pltpu.VMEM(flat, F32),
            pltpu.VMEM((2 * block, heads * width), BF16),
            pltpu.VMEM((heads, width, width), F32),
            pltpu.VMEM((bits, heads, width, width), BF16),
            pltpu.VMEM((bits, heads, width, width), BF16),
            pltpu.VMEM((bits, 8, 128), F32),
            pltpu.VMEM((bits, 8, 128), F32),
            pltpu.VMEM((heads, width, bits * width), BF16),
            pltpu.VMEM((chips,) + piece, BF16),
            pltpu.VMEM((chips,) + piece, BF16),
            pltpu.VMEM((chips - 1,) + piece, BF16),
            pltpu.VMEM(piece, BF16),
            dma((4,)),
            dma((bits, PARTS)),
            dma((bits, PARTS)),
            dma((bits,)),
            dma((bits,)),
            dma((chips, PIECES)),
            dma((chips, PIECES)),
            dma((chips - 1, PIECES)),
            dma((chips - 1, PIECES)),
            dma((PIECES,)),
        ],
        compiler_params=pltpu.CompilerParams(
            collective_id=0, has_side_effects=True, vmem_limit_bytes=58 * 1024 * 1024
        ),
    )(
        queries.reshape(flat),
        keys.reshape(flat),
        values.reshape(flat),
        out_weight,
        decay,
        weights,
        norm_gain,
    )
    mine = mine.astype(F32)
    for i in range(chips - 1):
        mine = mine + others[i].astype(F32)
    return mine.astype(BF16)


def solution(mesh):
    chips = mesh.shape["head"] // 2
    bits = mesh.shape["seq"].bit_length() - 1
    return jax.shard_map(
        functools.partial(body, chips, bits),
        mesh=mesh,
        in_specs=(
            P("seq", "head", None),
            P("seq", "head", None),
            P("seq", "head", None),
            P("seq", "head"),
            P("seq", "head", None),
            P("head", None),
            P("head", None),
        ),
        out_specs=P(("seq", "head"), None),
        check_vma=False,
    )
```
